512 devices in a mesh: wide: 32 (over x, y, z_hi), narrow: 16 (over z_lo, core).
Axes of the slice: x: 4, y: 4, z: 16 (z_hi: 2, z_lo: 8; z = z_hi * 8 + z_lo), core: 2. Of those that a mesh axis runs over, the one named last changes fastest.
Arguments:
- x_row_codes: bfloat16 [512, 18432], P(('narrow', 'wide')), may hold values from -3.75 to 3.75, as said below
- x_row_scales: int32 [512, 576], P(('narrow', 'wide')), may hold values from -2 to 1
- x_col_codes: bfloat16 [512, 18432], P(None, ('narrow', 'wide')), may hold values from -3.75 to 3.75, as said below
- x_col_scales: int32 [16, 18432], P(None, ('narrow', 'wide')), may hold values from -2 to 1
- grad_out: bfloat16 [512, 18432], P(('narrow', 'wide')), may hold values from -6 to 6
- up_weight: bfloat16 [18432, 8192], P('narrow', 'wide'), may hold values from -0.046875 to 0.046875
- down_weight: bfloat16 [8192, 18432], P('wide', 'narrow'), may hold values from -0.0625 to 0.0625
Outputs:
- input_grad: bfloat16 [512, 18432], P('wide', 'narrow')
- up_grad: float32 [18432, 8192], P('narrow', 'wide')
- down_grad: float32 [8192, 18432], P('wide', 'narrow')
The draws below stay inside these ranges and needn't reach their ends.
Inputs may be any that keep to these rules, and one draw needn't show every extreme that they name: `x_row_codes`: every entry is an E4M3 number s (1 + m/8) 2^e with s = -1 or 1, m of 0 to 7 and e of -3 to 1. `x_col_codes`: every entry is an E4M3 number s (1 + m/8) 2^e with s = -1 or 1, m of 0 to 7 and e of -3 to 1.
All inputs are finite; a program needn't handle non-finite values.
Results may differ from the reference program's by a relative error of at most 0.005.
Values may be sent and summed in bfloat16 or wider, within the bound.
No kernel may reach another device: no remote copies, remote signals or barrier semaphores. Data moves between devices by JAX's collectives and lax.ppermute only.
A program may use at most 64 MiB of HBM per device.

```python
import jax
import jax.numpy as jnp

D = 18432
FF = 8192
TOKENS = 512


def e4m3_values(key, shape):
    sign_key, mant_key, expo_key = jax.random.split(key, 3)
    signs = jax.random.randint(sign_key, shape, 0, 2) * 2 - 1
    mantissa = jax.random.randint(mant_key, shape, 0, 8)
    exponent = jax.random.randint(expo_key, shape, -3, 2)
    values = signs.astype(jnp.float32) * (1.0 + mantissa.astype(jnp.float32) / 8.0)
    return values * jnp.exp2(exponent.astype(jnp.float32))


def draw_x_row_codes(key, part):
    key = jax.random.fold_in(key, 11)
    return e4m3_values(key, (TOKENS, D)).astype(jnp.bfloat16)


def draw_x_col_codes(key, part):
    key = jax.random.fold_in(key, 23)
    return e4m3_values(key, (TOKENS, D)).astype(jnp.bfloat16)


def plant(array, rng, least, top_value):
    index_at = [jax.random.randint(jax.random.fold_in(rng, axis), (), 0, length) for axis, length in enumerate(array.shape)]
    widest = array.shape.index(max(array.shape))
    beside = index_at[:widest] + [(index_at[widest] + 1) % array.shape[widest]] + index_at[widest + 1:]
    return array.at[tuple(index_at)].set(least).at[tuple(beside)].set(top_value)


def levels(key, dims, shards, smallest, top_value):
    loudness = 1.0
    for axis_at, parts in shards:
        draws = jax.random.uniform(jax.random.fold_in(jax.random.fold_in(key, 6), axis_at), (parts,), jnp.float32, smallest / len(shards), top_value / len(shards))
        loudness = loudness * jnp.repeat(jnp.exp(draws), dims[axis_at] // parts).reshape((-1,) + (1,) * (len(dims) - 1 - axis_at))
    return loudness


def normal_values(rng, shape, scale, bound, pieces=(), held_as=jnp.bfloat16):
    array = jax.random.normal(rng, shape, jnp.float32) * scale
    if len(pieces) > 0:
        array = levels(rng, shape, pieces, -0.22, 0.18) * array
    return jnp.clip(array, min=-bound, max=bound).astype(held_as)


def setup_inputs(seed: int = 0) -> dict:
    streams_of = jax.random.split(jax.random.key(seed), 8)
    x_row_codes = draw_x_row_codes(jax.random.fold_in(streams_of[7], 71), 0)
    x_row_scales = plant(jax.random.randint(streams_of[1], (TOKENS, D // 32), -2, 2), jax.random.fold_in(streams_of[1], 1), -2, 1).astype(jnp.int32)
    x_col_codes = draw_x_col_codes(jax.random.fold_in(streams_of[7], 71), 0)
    x_col_scales = plant(jax.random.randint(streams_of[3], (TOKENS // 32, D), -2, 2), jax.random.fold_in(streams_of[3], 1), -2, 1).astype(jnp.int32)
    grad_out = normal_values(streams_of[4], (TOKENS, D), 1.0, 6.0, ((0, 512),))
    up_weight = normal_values(streams_of[5], (D, FF), D ** -0.5, 0.046875, ((0, 16), (1, 32)))
    down_weight = normal_values(streams_of[6], (FF, D), FF ** -0.5, 0.0625, ((0, 32), (1, 16)))
    return {"x_row_codes": x_row_codes, "x_row_scales": x_row_scales, "x_col_codes": x_col_codes, "x_col_scales": x_col_scales, "grad_out": grad_out, "up_weight": up_weight, "down_weight": down_weight}


def dequant_rows(codes, exps):
    tok_count, col_count = codes.shape
    blocks = codes.astype(jnp.float32).reshape(tok_count, col_count // 32, 32)
    blocks = blocks * jnp.exp2(exps.astype(jnp.float32))[:, :, None]
    return blocks.reshape(tok_count, col_count).astype(jnp.bfloat16)


def dequant_cols(codes, exps):
    tok_count, col_count = codes.shape
    blocks = codes.astype(jnp.float32).reshape(tok_count // 32, 32, col_count)
    blocks = blocks * jnp.exp2(exps.astype(jnp.float32))[:, None, :]
    return blocks.reshape(tok_count, col_count).astype(jnp.bfloat16)


def reference(x_row_codes, x_row_scales, x_col_codes, x_col_scales, grad_out, up_weight, down_weight):
    x_row = dequant_rows(x_row_codes, x_row_scales)
    x_col = dequant_cols(x_col_codes, x_col_scales)
    pre = jnp.dot(x_row, up_weight, preferred_element_type=jnp.float32)
    act_grad = jnp.dot(grad_out, down_weight.T, preferred_element_type=jnp.float32)
    positive = jnp.maximum(pre, 0.0)
    squared = (positive * positive).astype(jnp.bfloat16)
    hidden_grad = (act_grad * 2.0 * positive).astype(jnp.bfloat16)
    input_grad = jnp.dot(hidden_grad, up_weight.T, preferred_element_type=jnp.float32).astype(jnp.bfloat16)
    up_grad = jnp.dot(x_col.T, hidden_grad, preferred_element_type=jnp.float32)
    down_grad = jnp.dot(squared.T, grad_out, preferred_element_type=jnp.float32)
    return input_grad, up_grad, down_grad
```

```python
import jax
import jax.numpy as jnp
from jax import lax
from jax.sharding import Mesh
from jax.sharding import PartitionSpec as P

XY = ("x", "y")


def dequant_rows(codes, exps):
    tok_count, col_count = codes.shape
    blocks = codes.astype(jnp.float32).reshape(tok_count, col_count // 32, 32)
    blocks = blocks * jnp.exp2(exps.astype(jnp.float32))[:, :, None]
    return blocks.reshape(tok_count, col_count).astype(jnp.bfloat16)


def dequant_cols(codes, exps):
    tok_count, col_count = codes.shape
    blocks = codes.astype(jnp.float32).reshape(tok_count // 32, 32, col_count)
    blocks = blocks * jnp.exp2(exps.astype(jnp.float32))[:, None, :]
    return blocks.reshape(tok_count, col_count).astype(jnp.bfloat16)


def exchange(parts, axes):
    return lax.all_to_all(parts, axes, 0, 0)


def gather(part, axes, count):
    return exchange(jnp.broadcast_to(part[None], (count,) + part.shape), axes)


def other(part, axis):
    return lax.ppermute(part, axis, [(0, 1), (1, 0)])


def body(x_row_codes, x_row_scales, x_col_codes, x_col_scales, grad_out, up_weight, down_weight):
    bf16, f32 = jnp.bfloat16, jnp.float32
    width = up_weight.shape[0]
    core = lax.axis_index("c")
    z_hi = lax.axis_index("zh")

    x_row = dequant_rows(x_row_codes, x_row_scales)
    rows = jnp.stack([x_row.reshape(16, width), grad_out.reshape(16, width)], axis=1)
    rows = jnp.broadcast_to(rows[None], (2, 16, 2, width)).reshape(32, 2, width)
    rows = exchange(rows, ("zh", "zl", "c"))

    x_cols = gather(rows[:, 0], XY, 16).reshape(512, width)
    g_cols = gather(rows[:, 1], XY, 16).reshape(512, width)

    x_col = dequant_cols(x_col_codes, x_col_scales).T
    far = other(x_col, "zh")
    x_col = jnp.where(z_hi == 0, jnp.stack([x_col, far]), jnp.stack([far, x_col]))
    x_col = gather(x_col, XY, 16).reshape(width, 512)

    def reduce_narrow(part):
        part = part.reshape(8, 2, 32, 256)
        mine = lax.dynamic_index_in_dim(part, core, 1, keepdims=False)
        theirs = other(lax.dynamic_index_in_dim(part, 1 - core, 1, keepdims=False), "c")
        return exchange((mine + theirs).astype(bf16), "zl").astype(f32).sum(axis=0)

    pre = reduce_narrow(jnp.dot(x_cols, up_weight, preferred_element_type=f32))
    act_grad = reduce_narrow(jnp.einsum("td,fd->tf", g_cols, down_weight, preferred_element_type=f32))
    positive = jnp.maximum(pre, 0.0)
    squared = (positive * positive).astype(bf16)
    hidden_grad = (act_grad * 2.0 * positive).astype(bf16)

    both = gather(jnp.stack([hidden_grad, squared]), "zl", 8)
    far = other(both, "c")
    both = jnp.where(core == 0, jnp.stack([both, far], axis=1), jnp.stack([far, both], axis=1))
    squared = both[:, :, 1].reshape(512, 256)
    hidden_grad = both[:, :, 0].reshape(32, 16, 256).transpose(1, 0, 2).reshape(512, 256)

    part = jnp.einsum("tf,df->td", hidden_grad, up_weight, preferred_element_type=f32)
    part = exchange(part.astype(bf16).reshape(16, 32, width), XY).astype(f32).sum(axis=0)
    part = part.reshape(2, 16, width)
    mine = lax.dynamic_index_in_dim(part, z_hi, 0, keepdims=False)
    theirs = other(lax.dynamic_index_in_dim(part, 1 - z_hi, 0, keepdims=False), "zh")
    input_grad = (mine + theirs).astype(bf16)

    down_grad = jnp.einsum("tf,td->fd", squared, g_cols, preferred_element_type=f32)
    up_grad = jnp.dot(x_col, hidden_grad, preferred_element_type=f32)
    return (input_grad, up_grad, down_grad)


def solution(mesh):
    mesh = Mesh(mesh.devices.reshape(4, 4, 2, 8, 2), ("x", "y", "zh", "zl", "c"))
    wide, narrow = ("x", "y", "zh"), ("zl", "c")
    in_specs = (
        P(narrow + wide, None),
        P(narrow + wide, None),
        P(None, narrow + wide),
        P(None, narrow + wide),
        P(narrow + wide, None),
        P(narrow, wide),
        P(wide, narrow),
    )
    out_specs = (P(wide, narrow), P(narrow, wide), P(wide, narrow))
    return jax.shard_map(body, mesh=mesh, in_specs=in_specs, out_specs=out_specs, check_vma=False)
```

```python
import jax
import jax.numpy as jnp
from jax import lax
from jax.sharding import Mesh
from jax.sharding import PartitionSpec as P

XY = ("x", "y")
WIDE = ("x", "y", "zh")
NARROW = ("zl", "c")
F32 = jnp.float32
BF16 = jnp.bfloat16


def dequant_rows(codes, exps):
    tok_count, col_count = codes.shape
    blocks = codes.astype(F32).reshape(tok_count, col_count // 32, 32)
    blocks = blocks * jnp.exp2(exps.astype(F32))[:, :, None]
    return blocks.reshape(tok_count, col_count).astype(BF16)


def dequant_cols(codes, exps):
    tok_count, col_count = codes.shape
    blocks = codes.astype(F32).reshape(tok_count // 32, 32, col_count)
    blocks = blocks * jnp.exp2(exps.astype(F32))[:, None, :]
    return blocks.reshape(tok_count, col_count).astype(BF16)


def exchange(parts, axes):
    return lax.all_to_all(parts, axes, 0, 0)


def gather(part, axes, count):
    return exchange(jnp.broadcast_to(part[None], (count,) + part.shape), axes)


def partner(part, axis):
    return lax.ppermute(part, axis, [(0, 1), (1, 0)])


def pick(parts, index, axis=0):
    return lax.dynamic_index_in_dim(parts, index, axis, keepdims=False)


def in_order(index, own, far, axis=0):
    return jnp.where(index == 0, jnp.stack([own, far], axis), jnp.stack([far, own], axis))


def partial_sums(tokens, up, down):
    width = up[0].shape[0]
    x = [tokens[:, 0, k].reshape(256, width) for k in range(2)]
    g = [tokens[:, 1, k].reshape(256, width) for k in range(2)]
    pre = sum(jnp.dot(x[k], up[k], preferred_element_type=F32) for k in range(2))
    act = sum(jnp.einsum("td,fd->tf", g[k], down[k], preferred_element_type=F32) for k in range(2))
    return jnp.stack([pre, act]), g


def nonlinear(sums):
    positive = jnp.maximum(sums[0], 0.0)
    squared = (positive * positive).astype(BF16)
    hidden_grad = (sums[1] * 2.0 * positive).astype(BF16)
    return jnp.stack([squared, hidden_grad])


def body(x_row_codes, x_row_scales, x_col_codes, x_col_scales, grad_out, up_weight, down_weight):
    width = up_weight.shape[0]
    core, z_hi = (lax.axis_index(a) for a in ("c", "zh"))

    x_col = dequant_cols(x_col_codes, x_col_scales).T
    x_col = in_order(z_hi, x_col, partner(x_col, "zh"))
    up = (up_weight, partner(up_weight, "c"))
    down = (down_weight, partner(down_weight, "c"))

    x_row = dequant_rows(x_row_codes, x_row_scales)
    rows = jnp.stack([x_row.reshape(8, 2, width), grad_out.reshape(8, 2, width)], axis=1)
    rows = jnp.where(core == 0, rows, rows[:, :, ::-1])
    rows = jnp.broadcast_to(rows[None], (2,) + rows.shape).reshape(16, 2, 2, width)
    rows = exchange(rows, ("zh", "zl"))
    rows, up, down = lax.optimization_barrier((rows, up, down))
    rows = rows.transpose(1, 2, 0, 3)

    sums, g = partial_sums(gather(rows, XY, 16), up, down)
    g = jnp.concatenate([g[0], partner(g[1], "c")])

    part = exchange(sums.reshape(2, 8, 32, 256).transpose(1, 0, 2, 3).astype(BF16), "zl")
    part = nonlinear(part.astype(F32).sum(axis=0))
    own = gather(part, "zl", 8).transpose(1, 0, 2, 3).reshape(2, 256, 256)
    far = partner(own, "c")

    squared = jnp.concatenate([own[0], far[0]])
    hidden = in_order(core, own[1], far[1])
    hidden = hidden.reshape(2, 16, 2, 8, 256).transpose(3, 0, 1, 2, 4).reshape(512, 256)

    part = jnp.einsum("tf,df->td", hidden, up_weight, preferred_element_type=F32)
    part = exchange(part.astype(BF16).reshape(16, 32, width), XY).astype(F32).sum(axis=0).reshape(2, 16, width)
    down_grad = jnp.einsum("tf,td->fd", squared, g, preferred_element_type=F32)

    part, x_col = lax.optimization_barrier((part, x_col))
    theirs = partner(pick(part, 1 - z_hi).astype(BF16), "zh")
    x_col = gather(x_col, XY, 16).reshape(width, 512)
    up_grad = jnp.dot(x_col, hidden, preferred_element_type=F32)
    input_grad = (pick(part, z_hi) + theirs.astype(F32)).astype(BF16)
    return (input_grad, up_grad, down_grad)


def solution(mesh):
    mesh = Mesh(mesh.devices.reshape(4, 4, 2, 8, 2), ("x", "y", "zh", "zl", "c"))
    in_specs = (
        P(NARROW + WIDE, None),
        P(NARROW + WIDE, None),
        P(None, NARROW + WIDE),
        P(None, NARROW + WIDE),
        P(NARROW + WIDE, None),
        P(NARROW, WIDE),
        P(WIDE, NARROW),
    )
    out_specs = (P(WIDE, NARROW), P(NARROW, WIDE), P(WIDE, NARROW))
    return jax.shard_map(body, mesh=mesh, in_specs=in_specs, out_specs=out_specs, check_vma=False)
```

```python
import jax
import jax.numpy as jnp
from jax import lax
from jax.experimental import pallas as pl
from jax.experimental.pallas import tpu as pltpu
from jax.sharding import Mesh
from jax.sharding import PartitionSpec as P

XY = ("x", "y")
WIDE = ("x", "y", "zh")
NARROW = ("zl", "c")
F32 = jnp.float32
BF16 = jnp.bfloat16


def row_kernel(codes_in, exps_in, grad_in, out_ref, codes_ref, exps_ref, grad_ref, sems):
    moves = [
        pltpu.make_async_copy(source, to, sems.at[k])
        for k, (source, to) in enumerate(((codes_in, codes_ref), (exps_in, exps_ref), (grad_in, grad_ref)))
    ]
    for move in moves:
        move.start()
    for move in moves:
        move.wait()

    span = out_ref.shape[2]
    chips, blocks = out_ref.shape[0] // 2, span // 32
    exps = jnp.concatenate([exps_ref[:, i * blocks : (i + 1) * blocks] for i in range(chips)], axis=0)
    scales = jnp.exp2(exps.astype(F32)).astype(BF16)
    block_of = lax.broadcasted_iota(jnp.int32, (blocks, span), 1) // 32
    spread = (block_of == lax.broadcasted_iota(jnp.int32, (blocks, span), 0)).astype(BF16)
    scales = jnp.dot(scales, spread, preferred_element_type=F32)
    for i in range(chips):
        codes = codes_ref[:, i * span : (i + 1) * span].astype(F32)
        grad = grad_ref[:, i * span : (i + 1) * span].astype(F32)
        pair = jnp.concatenate([codes * scales[i : i + 1], grad], axis=0).astype(BF16)
        out_ref[i] = pair
        out_ref[chips + i] = pair


def rows_of(codes, exps, grad, chips):
    return pl.pallas_call(
        row_kernel,
        out_shape=jax.ShapeDtypeStruct((2 * chips, 2, codes.shape[1] // chips), BF16),
        in_specs=[pl.BlockSpec(memory_space=pl.ANY)] * 3,
        scratch_shapes=[pltpu.VMEM(a.shape, a.dtype) for a in (codes, exps, grad)] + [pltpu.SemaphoreType.DMA((3,))],
        compiler_params=pltpu.CompilerParams(vmem_limit_bytes=60 << 20),
        cost_estimate=pl.CostEstimate(flops=2 << 20, bytes_accessed=150 << 10, transcendentals=576),
    )(codes, exps, grad)


def sums_kernel(core_ref, tokens_ref, up_ref, far_up_ref, down_ref, far_down_ref, out_ref, g_ref, far_g_ref, *sum_refs):
    xy, rows, span = tokens_ref.shape
    half, width = rows // 2, span // 2

    def products(own, far):
        def part(first, own_ref, far_ref, dims):
            total = 0.0
            for side, ref in ((own, own_ref), (far, far_ref)):
                tokens = tokens_ref[:, first : first + half, side * width : (side + 1) * width]
                total += lax.dot_general(
                    tokens.reshape(xy * half, width), ref[...], (dims, ((), ())), preferred_element_type=F32
                )
            return total

        pre = part(0, up_ref, far_up_ref, ((1,), (0,)))
        act = part(half, down_ref, far_down_ref, ((1,), (1,)))
        g = tokens_ref[:, half:].reshape(xy * half, span)
        g_ref[...] = g[:, own * width : (own + 1) * width]
        far_g_ref[...] = g[:, far * width : (far + 1) * width]
        for k in range(2):
            sum_refs[k][...] = pre[:, k * 128 : (k + 1) * 128]
            sum_refs[2 + k][...] = act[:, k * 128 : (k + 1) * 128]

    @pl.when(core_ref[0] == 0)
    def _():
        products(0, 1)

    @pl.when(core_ref[0] == 1)
    def _():
        products(1, 0)

    for i in range(8):
        for k in range(4):
            out_ref[i, k // 2, :, k % 2 * 128 : (k % 2 + 1) * 128] = sum_refs[k][pl.ds(i, 32, stride=8), :].astype(BF16)


def partial_sums(core, tokens, up, far_up, down, far_down):
    hidden = up.shape[1]
    count = tokens.shape[0] * tokens.shape[1] // 2
    vmem = pl.BlockSpec(memory_space=pltpu.VMEM)
    return pl.pallas_call(
        sums_kernel,
        out_shape=[jax.ShapeDtypeStruct((8, 2, count // 8, hidden), BF16)]
        + [jax.ShapeDtypeStruct((count, up.shape[0]), BF16)] * 2,
        in_specs=[pl.BlockSpec(memory_space=pltpu.SMEM)] + [vmem] * 5,
        out_specs=[vmem] * 3,
        scratch_shapes=[pltpu.VMEM((count, 128), F32)] * 4,
        compiler_params=pltpu.CompilerParams(vmem_limit_bytes=48 << 20),
        cost_estimate=pl.CostEstimate(flops=2 * tokens.size * hidden, bytes_accessed=5 << 20, transcendentals=0),
    )(core.reshape(1), tokens, up, far_up, down, far_down)


def share_kernel(core_ref, own_ref, far_ref, up_ref, out_ref, hidden_ref):
    @pl.when(core_ref[0] == 0)
    def _():
        hidden_ref[:, 0] = own_ref[:, 1]
        hidden_ref[:, 1] = far_ref[:, 1]

    @pl.when(core_ref[0] == 1)
    def _():
        hidden_ref[:, 0] = far_ref[:, 1]
        hidden_ref[:, 1] = own_ref[:, 1]

    hidden = hidden_ref[...].reshape(512, up_ref.shape[1])
    part = lax.dot_general(hidden, up_ref[...], (((1,), (1,)), ((), ())), preferred_element_type=F32)
    out_ref[...] = part.astype(BF16).reshape(out_ref.shape)


def shares(core, own, far, up):
    vmem = pl.BlockSpec(memory_space=pltpu.VMEM)
    return pl.pallas_call(
        share_kernel,
        out_shape=[
            jax.ShapeDtypeStruct((16, 32, up.shape[0]), BF16),
            jax.ShapeDtypeStruct((8, 2, 32, up.shape[1]), BF16),
        ],
        in_specs=[pl.BlockSpec(memory_space=pltpu.SMEM)] + [vmem] * 3,
        out_specs=[vmem] * 2,
        compiler_params=pltpu.CompilerParams(vmem_limit_bytes=32 << 20),
        cost_estimate=pl.CostEstimate(flops=1024 * up.size, bytes_accessed=3 << 20, transcendentals=0),
    )(core.reshape(1), own, far, up)


def dequant_cols(codes, exps):
    tok_count, col_count = codes.shape
    blocks = codes.astype(F32).reshape(tok_count // 32, 32, col_count)
    blocks = blocks * jnp.exp2(exps.astype(F32))[:, None, :]
    return blocks.reshape(tok_count, col_count).astype(BF16)


def exchange(parts, axes):
    return lax.all_to_all(parts, axes, 0, 0)


def gather(part, axes, count):
    return exchange(jnp.broadcast_to(part[None], (count,) + part.shape), axes)


def partner(part, axis):
    return lax.ppermute(part, axis, [(0, 1), (1, 0)])


def pick(parts, index, axis=0):
    return lax.dynamic_index_in_dim(parts, index, axis, keepdims=False)


def in_order(index, own, far, axis=0):
    return jnp.where(index == 0, jnp.stack([own, far], axis), jnp.stack([far, own], axis))


def nonlinear(sums):
    positive = jnp.maximum(sums[0], 0.0)
    squared = (positive * positive).astype(BF16)
    hidden_grad = (sums[1] * 2.0 * positive).astype(BF16)
    return jnp.stack([squared, hidden_grad])


def body(x_row_codes, x_row_scales, x_col_codes, x_col_scales, grad_out, up_weight, down_weight):
    width = up_weight.shape[0]
    core, z_hi = (lax.axis_index(a) for a in ("c", "zh"))

    rows = exchange(rows_of(x_row_codes, x_row_scales, grad_out, 8), ("zh", "zl"))
    rows = rows.transpose(1, 0, 2).reshape(32, 2 * width)

    x_col = dequant_cols(x_col_codes, x_col_scales).T
    rows, x_col, up, down = lax.optimization_barrier((rows, x_col, up_weight, down_weight))
    x_col = in_order(z_hi, x_col, partner(x_col, "zh"))
    far_up, far_down = partner(up, "c"), partner(down, "c")

    tokens = gather(rows, XY, 16)
    tokens, far_up, far_down, x_col = lax.optimization_barrier((tokens, far_up, far_down, x_col))
    sums, g, far_g = partial_sums(core, tokens, up, far_up, down, far_down)
    far_g, x_col = lax.optimization_barrier((far_g, jnp.broadcast_to(x_col[None], (16,) + x_col.shape)))
    g = jnp.concatenate([g, partner(far_g, "c")])

    part = exchange(sums, "zl").astype(F32).sum(axis=0)
    own = gather(nonlinear(part), "zl", 8)
    far = partner(own, "c")

    part, hidden = shares(core, own, far, up_weight)
    part = exchange(part, XY).astype(F32).sum(axis=0).reshape(2, 16, width)

    part, x_col = lax.optimization_barrier((part, x_col))
    theirs = partner(pick(part, 1 - z_hi).astype(BF16), "zh")
    x_col = exchange(x_col, XY).reshape(width, 512)
    up_grad = jnp.dot(x_col, hidden.reshape(512, 256), preferred_element_type=F32)
    input_grad = (pick(part, z_hi) + theirs.astype(F32)).astype(BF16)

    squared = jnp.stack([own[:, 0], far[:, 0]]).transpose(0, 2, 1, 3).reshape(512, 256)
    down_grad = jnp.einsum("tf,td->fd", squared, g, preferred_element_type=F32)
    return (input_grad, up_grad, down_grad)


def solution(mesh):
    mesh = Mesh(mesh.devices.reshape(4, 4, 2, 8, 2), ("x", "y", "zh", "zl", "c"))
    in_specs = (
        P(NARROW + WIDE, None),
        P(NARROW + WIDE, None),
        P(None, NARROW + WIDE),
        P(None, NARROW + WIDE),
        P(NARROW + WIDE, None),
        P(NARROW, WIDE),
        P(WIDE, NARROW),
    )
    out_specs = (P(WIDE, NARROW), P(NARROW, WIDE), P(WIDE, NARROW))
    return jax.shard_map(body, mesh=mesh, in_specs=in_specs, out_specs=out_specs, check_vma=False)
```

```python
import jax
import jax.numpy as jnp
from jax import lax
from jax.experimental import pallas as pl
from jax.experimental.pallas import tpu as pltpu
from jax.sharding import Mesh
from jax.sharding import PartitionSpec as P

XY = ("x", "y")
WIDE = ("x", "y", "zh")
NARROW = ("zl", "c")
F32 = jnp.float32
BF16 = jnp.bfloat16


def row_kernel(codes_in, exps_in, grad_in, out_ref, codes_ref, exps_ref, grad_ref, sems):
    moves = [
        pltpu.make_async_copy(source, to, sems.at[k])
        for k, (source, to) in enumerate(((codes_in, codes_ref), (exps_in, exps_ref), (grad_in, grad_ref)))
    ]
    for move in moves:
        move.start()

    span = out_ref.shape[2]
    chips, blocks = out_ref.shape[0] // 2, span // 32
    block_of = lax.broadcasted_iota(jnp.int32, (blocks, span), 1) // 32
    spread = (block_of == lax.broadcasted_iota(jnp.int32, (blocks, span), 0)).astype(BF16)
    moves[1].wait()
    exps = jnp.concatenate([exps_ref[:, i * blocks : (i + 1) * blocks] for i in range(chips)], axis=0)
    scales = jnp.exp2(exps.astype(F32)).astype(BF16)
    scales = jnp.dot(scales, spread, preferred_element_type=F32)
    moves[0].wait()
    moves[2].wait()
    for i in range(chips):
        codes = codes_ref[:, i * span : (i + 1) * span].astype(F32)
        grad = grad_ref[:, i * span : (i + 1) * span].astype(F32)
        pair = jnp.concatenate([codes * scales[i : i + 1], grad], axis=0).astype(BF16)
        out_ref[i] = pair
        out_ref[chips + i] = pair


def rows_of(codes, exps, grad, chips):
    return pl.pallas_call(
        row_kernel,
        out_shape=jax.ShapeDtypeStruct((2 * chips, 2, codes.shape[1] // chips), BF16),
        in_specs=[pl.BlockSpec(memory_space=pl.ANY)] * 3,
        scratch_shapes=[pltpu.VMEM(a.shape, a.dtype) for a in (codes, exps, grad)] + [pltpu.SemaphoreType.DMA((3,))],
        compiler_params=pltpu.CompilerParams(vmem_limit_bytes=60 << 20),
        cost_estimate=pl.CostEstimate(flops=2 << 20, bytes_accessed=150 << 10, transcendentals=576),
    )(codes, exps, grad)


def sums_kernel(tokens_ref, up_ref, far_up_in, down_ref, far_down_in, out_ref, g_ref, far_g_ref, *scratch):
    far_up_ref, far_down_ref, sems = scratch
    moves = [
        pltpu.make_async_copy(source, to, sems.at[k])
        for k, (source, to) in enumerate(((far_up_in, far_up_ref), (far_down_in, far_down_ref)))
    ]
    for move in moves:
        move.start()
    xy, rows, span = tokens_ref.shape
    half, width = rows // 2, span // 2
    count = xy * half
    to = lax.broadcasted_iota(jnp.int32, (count, count), 0)
    source = lax.broadcasted_iota(jnp.int32, (count, count), 1)
    order = (source == to % (count // 8) * 8 + to // (count // 8)).astype(BF16)

    core = lax.axis_index("c")
    own, far = (pl.ds(pl.multiple_of(side * width, 128), width) for side in (core, 1 - core))

    def part(first, columns, ref, dims):
        tokens = tokens_ref[:, first : first + half, columns].reshape(count, width)
        return lax.dot_general(tokens, ref[...], (dims, ((), ())), preferred_element_type=F32)

    pre = part(0, own, up_ref, ((1,), (0,)))
    act = part(half, own, down_ref, ((1,), (1,)))
    g_ref[...] = tokens_ref[:, half:, own].reshape(count, width)
    far_g_ref[...] = tokens_ref[:, half:, far].reshape(count, width)
    for move in moves:
        move.wait()
    pre += part(0, far, far_up_ref, ((1,), (0,)))
    act += part(half, far, far_down_ref, ((1,), (1,)))
    for k, total in enumerate((pre, act)):
        total = jnp.dot(order, total.astype(BF16), preferred_element_type=F32)
        out_ref[:, k] = total.astype(BF16).reshape(8, count // 8, total.shape[1])


def partial_sums(tokens, up, far_up, down, far_down):
    hidden = up.shape[1]
    count = tokens.shape[0] * tokens.shape[1] // 2
    vmem, anywhere = pl.BlockSpec(memory_space=pltpu.VMEM), pl.BlockSpec(memory_space=pl.ANY)
    return pl.pallas_call(
        sums_kernel,
        out_shape=[jax.ShapeDtypeStruct((8, 2, count // 8, hidden), BF16)]
        + [jax.ShapeDtypeStruct((count, up.shape[0]), BF16)] * 2,
        in_specs=[vmem, vmem, anywhere, vmem, anywhere],
        out_specs=[vmem] * 3,
        scratch_shapes=[pltpu.VMEM(far_up.shape, BF16), pltpu.VMEM(far_down.shape, BF16), pltpu.SemaphoreType.DMA((2,))],
        compiler_params=pltpu.CompilerParams(vmem_limit_bytes=48 << 20),
        cost_estimate=pl.CostEstimate(flops=2 * tokens.size * hidden, bytes_accessed=5 << 20, transcendentals=0),
    )(tokens, up, far_up, down, far_down)


def share_kernel(own_ref, far_ref, up_ref, out_ref, hidden_ref):
    @pl.when(lax.axis_index("c") == 0)
    def _():
        hidden_ref[:, 0] = own_ref[:, 1]
        hidden_ref[:, 1] = far_ref[:, 1]

    @pl.when(lax.axis_index("c") == 1)
    def _():
        hidden_ref[:, 0] = far_ref[:, 1]
        hidden_ref[:, 1] = own_ref[:, 1]

    hidden = hidden_ref[...].reshape(512, up_ref.shape[1])
    part = lax.dot_general(hidden, up_ref[...], (((1,), (1,)), ((), ())), preferred_element_type=F32)
    out_ref[...] = part.astype(BF16).reshape(out_ref.shape)


def shares(own, far, up):
    vmem = pl.BlockSpec(memory_space=pltpu.VMEM)
    return pl.pallas_call(
        share_kernel,
        out_shape=[
            jax.ShapeDtypeStruct((16, 32, up.shape[0]), BF16),
            jax.ShapeDtypeStruct((8, 2, 32, up.shape[1]), BF16),
        ],
        in_specs=[vmem] * 3,
        out_specs=[vmem] * 2,
        compiler_params=pltpu.CompilerParams(vmem_limit_bytes=32 << 20),
        cost_estimate=pl.CostEstimate(flops=1024 * up.size, bytes_accessed=3 << 20, transcendentals=0),
    )(own, far, up)


def dequant_cols(codes, exps):
    tok_count, col_count = codes.shape
    blocks = codes.astype(F32).reshape(tok_count // 32, 32, col_count)
    blocks = blocks * jnp.exp2(exps.astype(F32))[:, None, :]
    return blocks.reshape(tok_count, col_count).astype(BF16)


def exchange(parts, axes):
    return lax.all_to_all(parts, axes, 0, 0)


def gather(part, axes, count):
    return exchange(jnp.broadcast_to(part[None], (count,) + part.shape), axes)


def partner(part, axis):
    return lax.ppermute(part, axis, [(0, 1), (1, 0)])


def pick(parts, index, axis=0):
    return lax.dynamic_index_in_dim(parts, index, axis, keepdims=False)


def in_order(index, own, far, axis=0):
    return jnp.where(index == 0, jnp.stack([own, far], axis), jnp.stack([far, own], axis))


def nonlinear(sums):
    positive = jnp.maximum(sums[0], 0.0)
    squared = (positive * positive).astype(BF16)
    hidden_grad = (sums[1] * 2.0 * positive).astype(BF16)
    return jnp.stack([squared, hidden_grad])


def body(x_row_codes, x_row_scales, x_col_codes, x_col_scales, grad_out, up_weight, down_weight):
    width = up_weight.shape[0]
    z_hi = lax.axis_index("zh")

    rows = exchange(rows_of(x_row_codes, x_row_scales, grad_out, 8), ("zh", "zl"))
    rows = rows.transpose(1, 0, 2).reshape(32, 2 * width)

    x_col = dequant_cols(x_col_codes, x_col_scales).T
    rows, x_col, up, down = lax.optimization_barrier((rows, x_col, up_weight, down_weight))
    x_col = in_order(z_hi, x_col, partner(x_col, "zh"))
    far_up, far_down = partner(up, "c"), partner(down, "c")

    tokens = gather(rows, XY, 16)
    tokens, far_up, far_down, x_col = lax.optimization_barrier((tokens, far_up, far_down, x_col))
    sums, g, far_g = partial_sums(tokens, up, far_up, down, far_down)
    far_g, x_col = lax.optimization_barrier((far_g, jnp.broadcast_to(x_col[None], (16,) + x_col.shape)))
    g = jnp.concatenate([g, partner(far_g, "c")])

    part = exchange(sums, "zl").astype(F32).sum(axis=0)
    own = gather(nonlinear(part), "zl", 8)
    far = partner(own, "c")

    part, hidden = shares(own, far, up_weight)
    part = exchange(part, XY).astype(F32).sum(axis=0).reshape(2, 16, width)

    part, x_col = lax.optimization_barrier((part, x_col))
    theirs = partner(pick(part, 1 - z_hi).astype(BF16), "zh")
    x_col = exchange(x_col, XY).reshape(width, 512)
    up_grad = jnp.dot(x_col, hidden.reshape(512, 256), preferred_element_type=F32)
    input_grad = (pick(part, z_hi) + theirs.astype(F32)).astype(BF16)

    squared = jnp.stack([own[:, 0], far[:, 0]]).transpose(0, 2, 1, 3).reshape(512, 256)
    down_grad = jnp.einsum("tf,td->fd", squared, g, preferred_element_type=F32)
    return (input_grad, up_grad, down_grad)


def solution(mesh):
    mesh = Mesh(mesh.devices.reshape(4, 4, 2, 8, 2), ("x", "y", "zh", "zl", "c"))
    in_specs = (
        P(NARROW + WIDE, None),
        P(NARROW + WIDE, None),
        P(None, NARROW + WIDE),
        P(None, NARROW + WIDE),
        P(NARROW + WIDE, None),
        P(NARROW, WIDE),
        P(WIDE, NARROW),
    )
    out_specs = (P(WIDE, NARROW), P(NARROW, WIDE), P(WIDE, NARROW))
    return jax.shard_map(body, mesh=mesh, in_specs=in_specs, out_specs=out_specs, check_vma=False)
```

```python
import jax
import jax.numpy as jnp
from jax import lax
from jax.experimental import pallas as pl
from jax.experimental.pallas import tpu as pltpu
from jax.sharding import Mesh
from jax.sharding import PartitionSpec as P

XY = ("x", "y")
WIDE = ("x", "y", "zh")
NARROW = ("zl", "c")
F32 = jnp.float32
BF16 = jnp.bfloat16


def row_kernel(codes_in, exps_in, grad_in, out_ref, codes_ref, exps_ref, grad_ref, sems):
    moves = [
        pltpu.make_async_copy(source, to, sems.at[k])
        for k, (source, to) in enumerate(((codes_in, codes_ref), (exps_in, exps_ref), (grad_in, grad_ref)))
    ]
    for move in moves:
        move.start()

    span = out_ref.shape[2]
    chips, blocks = out_ref.shape[0] // 2, span // 32
    block_of = lax.broadcasted_iota(jnp.int32, (blocks, span), 1) // 32
    spread = (block_of == lax.broadcasted_iota(jnp.int32, (blocks, span), 0)).astype(BF16)
    moves[1].wait()
    exps = jnp.concatenate([exps_ref[:, i * blocks : (i + 1) * blocks] for i in range(chips)], axis=0)
    scales = jnp.exp2(exps.astype(F32)).astype(BF16)
    scales = jnp.dot(scales, spread, preferred_element_type=F32)
    moves[0].wait()
    moves[2].wait()
    for i in range(chips):
        codes = codes_ref[:, i * span : (i + 1) * span].astype(F32)
        grad = grad_ref[:, i * span : (i + 1) * span].astype(F32)
        pair = jnp.concatenate([codes * scales[i : i + 1], grad], axis=0).astype(BF16)
        out_ref[i] = pair
        out_ref[chips + i] = pair


def rows_of(codes, exps, grad, chips):
    return pl.pallas_call(
        row_kernel,
        out_shape=jax.ShapeDtypeStruct((2 * chips, 2, codes.shape[1] // chips), BF16),
        in_specs=[pl.BlockSpec(memory_space=pl.ANY)] * 3,
        scratch_shapes=[pltpu.VMEM(a.shape, a.dtype) for a in (codes, exps, grad)] + [pltpu.SemaphoreType.DMA((3,))],
        compiler_params=pltpu.CompilerParams(vmem_limit_bytes=60 << 20),
        cost_estimate=pl.CostEstimate(flops=2 << 20, bytes_accessed=150 << 10, transcendentals=576),
    )(codes, exps, grad)


def sums_kernel(tokens_ref, up_ref, far_up_in, down_ref, far_down_in, out_ref, g_ref, far_g_ref, *scratch):
    far_up_ref, far_down_ref, sems = scratch
    moves = [
        pltpu.make_async_copy(source, to, sems.at[k])
        for k, (source, to) in enumerate(((far_up_in, far_up_ref), (far_down_in, far_down_ref)))
    ]
    for move in moves:
        move.start()
    xy, rows, span = tokens_ref.shape
    half, width = rows // 2, span // 2
    count = xy * half
    to = lax.broadcasted_iota(jnp.int32, (count, count), 0)
    source = lax.broadcasted_iota(jnp.int32, (count, count), 1)
    order = (source == to % (count // 8) * 8 + to // (count // 8)).astype(BF16)

    core = lax.axis_index("c")
    own, far = (pl.ds(pl.multiple_of(side * width, 128), width) for side in (core, 1 - core))

    def part(first, columns, ref, dims):
        tokens = tokens_ref[:, first : first + half, columns].reshape(count, width)
        return lax.dot_general(tokens, ref[...], (dims, ((), ())), preferred_element_type=F32)

    pre = part(0, own, up_ref, ((1,), (0,)))
    act = part(half, own, down_ref, ((1,), (1,)))
    g_ref[...] = tokens_ref[:, half:, own].reshape(count, width)
    far_g_ref[...] = tokens_ref[:, half:, far].reshape(count, width)
    for move in moves:
        move.wait()
    pre += part(0, far, far_up_ref, ((1,), (0,)))
    act += part(half, far, far_down_ref, ((1,), (1,)))
    for k, total in enumerate((pre, act)):
        total = jnp.dot(order, total.astype(BF16), preferred_element_type=F32)
        out_ref[:, k] = total.astype(BF16).reshape(8, count // 8, total.shape[1])


def partial_sums(tokens, up, far_up, down, far_down):
    hidden = up.shape[1]
    count = tokens.shape[0] * tokens.shape[1] // 2
    vmem, anywhere = pl.BlockSpec(memory_space=pltpu.VMEM), pl.BlockSpec(memory_space=pl.ANY)
    return pl.pallas_call(
        sums_kernel,
        out_shape=[jax.ShapeDtypeStruct((8, 2, count // 8, hidden), BF16)]
        + [jax.ShapeDtypeStruct((count, up.shape[0]), BF16)] * 2,
        in_specs=[vmem, vmem, anywhere, vmem, anywhere],
        out_specs=[vmem] * 3,
        scratch_shapes=[pltpu.VMEM(far_up.shape, BF16), pltpu.VMEM(far_down.shape, BF16), pltpu.SemaphoreType.DMA((2,))],
        compiler_params=pltpu.CompilerParams(vmem_limit_bytes=48 << 20),
        cost_estimate=pl.CostEstimate(flops=2 * tokens.size * hidden, bytes_accessed=5 << 20, transcendentals=0),
    )(tokens, up, far_up, down, far_down)


def share_kernel(own_ref, far_ref, up_ref, out_ref, hidden_ref):
    core = lax.axis_index("c")
    hidden_ref[:, core] = own_ref[:, 1]
    hidden_ref[:, 1 - core] = far_ref[:, 1]

    hidden = hidden_ref[...].reshape(512, up_ref.shape[1])
    part = lax.dot_general(hidden, up_ref[...], (((1,), (1,)), ((), ())), preferred_element_type=F32)
    out_ref[...] = part.astype(BF16).reshape(out_ref.shape)


def shares(own, far, up):
    vmem = pl.BlockSpec(memory_space=pltpu.VMEM)
    return pl.pallas_call(
        share_kernel,
        out_shape=[
            jax.ShapeDtypeStruct((16, 32, up.shape[0]), BF16),
            jax.ShapeDtypeStruct((8, 2, 32, up.shape[1]), BF16),
        ],
        in_specs=[vmem] * 3,
        out_specs=[vmem] * 2,
        compiler_params=pltpu.CompilerParams(vmem_limit_bytes=32 << 20),
        cost_estimate=pl.CostEstimate(flops=1024 * up.size, bytes_accessed=3 << 20, transcendentals=0),
    )(own, far, up)


def dequant_cols(codes, exps):
    tok_count, col_count = codes.shape
    blocks = codes.astype(F32).reshape(tok_count // 32, 32, col_count)
    blocks = blocks * jnp.exp2(exps.astype(F32))[:, None, :]
    return blocks.reshape(tok_count, col_count).astype(BF16)


def exchange(parts, axes):
    return lax.all_to_all(parts, axes, 0, 0)


def gather(part, axes, count):
    return exchange(jnp.broadcast_to(part[None], (count,) + part.shape), axes)


def partner(part, axis):
    return lax.ppermute(part, axis, [(0, 1), (1, 0)])


def pick(parts, index, axis=0):
    return lax.dynamic_index_in_dim(parts, index, axis, keepdims=False)


def in_order(index, own, far, axis=0):
    return jnp.where(index == 0, jnp.stack([own, far], axis), jnp.stack([far, own], axis))


def nonlinear(sums):
    positive = jnp.maximum(sums[0], 0.0)
    squared = (positive * positive).astype(BF16)
    hidden_grad = (sums[1] * 2.0 * positive).astype(BF16)
    return jnp.stack([squared, hidden_grad])


def body(x_row_codes, x_row_scales, x_col_codes, x_col_scales, grad_out, up_weight, down_weight):
    width = up_weight.shape[0]
    z_hi = lax.axis_index("zh")

    rows = exchange(rows_of(x_row_codes, x_row_scales, grad_out, 8), ("zh", "zl"))
    rows = rows.transpose(1, 0, 2).reshape(32, 2 * width)

    x_col = dequant_cols(x_col_codes, x_col_scales).T
    rows, x_col, up, down = lax.optimization_barrier((rows, x_col, up_weight, down_weight))
    x_col = in_order(z_hi, x_col, partner(x_col, "zh"))
    far_up, far_down = partner(up, "c"), partner(down, "c")

    tokens = gather(rows, XY, 16)
    tokens, far_up, far_down, x_col = lax.optimization_barrier((tokens, far_up, far_down, x_col))
    sums, g, far_g = partial_sums(tokens, up, far_up, down, far_down)
    far_g, x_col = lax.optimization_barrier((far_g, jnp.broadcast_to(x_col[None], (16,) + x_col.shape)))
    g = jnp.concatenate([g, partner(far_g, "c")])

    part = exchange(sums, "zl").astype(F32).sum(axis=0)
    own = gather(nonlinear(part), "zl", 8)
    far = partner(own, "c")

    part, hidden = shares(own, far, up_weight)
    part = exchange(part, XY).astype(F32).sum(axis=0).reshape(2, 16, width)

    part, x_col = lax.optimization_barrier((part, x_col))
    theirs = partner(pick(part, 1 - z_hi).astype(BF16), "zh")
    x_col = exchange(x_col, XY).reshape(width, 512)
    up_grad = jnp.dot(x_col, hidden.reshape(512, 256), preferred_element_type=F32)
    input_grad = (pick(part, z_hi) + theirs.astype(F32)).astype(BF16)

    squared = jnp.stack([own[:, 0], far[:, 0]]).transpose(0, 2, 1, 3).reshape(512, 256)
    down_grad = jnp.einsum("tf,td->fd", squared, g, preferred_element_type=F32)
    return (input_grad, up_grad, down_grad)


def solution(mesh):
    mesh = Mesh(mesh.devices.reshape(4, 4, 2, 8, 2), ("x", "y", "zh", "zl", "c"))
    in_specs = (
        P(NARROW + WIDE, None),
        P(NARROW + WIDE, None),
        P(None, NARROW + WIDE),
        P(None, NARROW + WIDE),
        P(NARROW + WIDE, None),
        P(NARROW, WIDE),
        P(WIDE, NARROW),
    )
    out_specs = (P(WIDE, NARROW), P(NARROW, WIDE), P(WIDE, NARROW))
    return jax.shard_map(body, mesh=mesh, in_specs=in_specs, out_specs=out_specs, check_vma=False)
```
